256 devices in a mesh: tm: 8 (over y_hi, x), row: 32 (over y_lo, z, core).
Axes of the slice: x: 4, y: 4 (y_hi: 2, y_lo: 2; y = y_hi * 2 + y_lo), z: 8, core: 2. Of those that a mesh axis runs over, the one named last changes fastest.
Arguments:
- field: float32 [1, 2048, 16384], P(None, 'row', 'tm'), may hold values from -6 to 6
- screen: float32 [1, 2048], P(None, 'row'), may hold values from -1.8 to 1.8
Outputs:
- spectrum: float32 [2, 1, 8192, 2048], P(None, None, ('tm', 'row'))
The draws below stay inside these ranges and needn't reach their ends.
All inputs are finite; a program needn't handle non-finite values.
Results may differ from the reference program's by a relative error of at most 0.00024.
Values sent between devices are 32-bit elements; how exact they have to be, the bound alone decides.
No kernel may reach another device: no remote copies, remote signals or barrier semaphores. Data moves between devices by JAX's collectives and lax.ppermute only.
A program may use at most 64 MiB of HBM per device.

```python
import math
import jax
import jax.numpy as jnp
from jax import lax

NX = 2048
NT = 16384
ROWS = 1
NF = 8192


def level_of(own_key, dims, cuts, low, high):
    def one(position, parts):
        steps = jax.random.uniform(jax.random.fold_in(jax.random.fold_in(own_key, 6), position), (parts,), jnp.float32, low / len(cuts), high / len(cuts))
        return jnp.repeat(jnp.exp(steps), dims[position] // parts).reshape((-1,) + (1,) * (len(dims) - position - 1))

    factor_of = one(*cuts[0])
    for cut in cuts[1:]:
        factor_of = factor_of * one(*cut)
    return factor_of


def scatter_about(key, shape, width, most, split=(), kind=jnp.bfloat16):
    array = width * jax.random.normal(key, shape, jnp.float32)
    if split:
        array = array * level_of(key, shape, split, -0.22, 0.18)
    return jnp.clip(array, -most, most).astype(kind)


def setup_inputs(seed: int = 0) -> dict:
    arg_keys = jax.random.split(jax.random.key(seed), 3)
    return {
        "field": scatter_about(arg_keys[0], (ROWS, NX, NT), 1.0, 6.0, ((1, 32), (2, 8)), jnp.float32),
        "screen": scatter_about(arg_keys[1], (ROWS, NX), 0.3, 1.8, ((1, 32),), jnp.float32),
    }


kerr_coeff = 0.3
ionize_rate = 0.4

def source_weights(scaled):
    return (0.2 * scaled, 0.5 / (1.0 + 64.0 * scaled * scaled))

def phase_angle(scaled, transverse):
    return 40.0 * scaled * (1.0 + 0.3 * scaled * scaled) - 20.0 * transverse * transverse / (scaled + 0.05)

def reference(field, screen):
    freq_index = jnp.arange(NF, dtype=jnp.int32)
    scaled = freq_index.astype(jnp.float32) / NF
    weight_kerr, weight_plasma = source_weights(scaled)
    kx_index = jnp.arange(NX, dtype=jnp.int32)
    transverse = jnp.where(kx_index < NX // 2, kx_index, kx_index - NX).astype(jnp.float32) / (NX // 2)
    phase_table = phase_angle(scaled[:, None], transverse[None, :])
    propagator = jnp.cos(phase_table) + 1j * jnp.sin(phase_table)

    def spectrum_of(values):
        return jnp.fft.rfft(values, axis=1)[:, :NF] / math.sqrt(NT)

    def one_row(row_item):
        sample, screen_row = row_item
        fourth_power = sample ** 4
        density = ionize_rate / NT * jnp.cumsum(fourth_power, axis=1)
        polarization = kerr_coeff * sample ** 3 + 2.0 * screen_row[:, None] * sample
        current = density * sample
        combined = spectrum_of(sample) + 1j * weight_kerr * spectrum_of(polarization) - weight_plasma * spectrum_of(current)
        across = jnp.fft.fft(combined, axis=0) / math.sqrt(NX)
        turned = across.T * propagator
        return jnp.stack([jnp.real(turned), jnp.imag(turned)]).astype(jnp.float32)
    result = lax.map(one_row, (field, screen))
    return jnp.transpose(result, (1, 0, 2, 3))
```

```python
import math

import jax
import jax.numpy as jnp
import ml_dtypes
import numpy as np
from jax import lax
from jax.experimental import pallas as pl
from jax.experimental.pallas import tpu as pltpu
from jax.sharding import PartitionSpec as P

NX = 2048
NT = 16384
NF = 8192

kerr_coeff = 0.3
ionize_rate = 0.4

F32 = jnp.float32
BF16 = jnp.bfloat16


def two_parts(table):
    high = table.astype(ml_dtypes.bfloat16)
    low = (table - high.astype(np.float64)).astype(ml_dtypes.bfloat16)
    return high, low


def turns(left, right, period):
    product = (np.asarray(left)[:, None] * np.asarray(right)[None, :]) % period
    angle = product.astype(np.float64) * (2.0 * math.pi / period)
    return np.cos(angle), np.sin(angle)


def time_tables():
    index = np.arange(128)
    cos_one, sin_one = turns(index, index, 128)
    one_high, one_low = two_parts(np.concatenate([cos_one, -sin_one], 0))
    one = np.concatenate([one_high, one_high, one_low], 1)
    cos_twist, sin_twist = turns(index, index, NT)
    twist = np.stack([cos_twist, sin_twist]).astype(np.float32)
    cos_two, sin_two = turns(np.arange(64), index, 128)
    scale = 1.0 / math.sqrt(NT)
    two = np.block([[cos_two, sin_two], [-sin_two, cos_two]]) * scale
    two_high, two_low = two_parts(two)
    two = np.concatenate([two_high, two_low], 0)
    within = (index[:, None] <= index[None, :]).astype(np.float64)
    within = np.concatenate([within, np.ones((128, 128))], 1)
    within = np.concatenate([within, within], 0).astype(ml_dtypes.bfloat16)
    earlier = (index[None, :] < index[:, None]).astype(np.float64)
    earlier = np.concatenate([earlier, earlier], 1).astype(ml_dtypes.bfloat16)
    return one, twist, two, within, earlier


def cross_tables():
    order = np.arange(128)
    x_hi = (order % 32) * 4 + order // 32
    cos_one, sin_one = turns(x_hi, np.arange(128), 128)
    scale = 1.0 / math.sqrt(NX)
    table = np.block([[cos_one, -sin_one], [sin_one, cos_one]]) * scale
    high, low = two_parts(table)
    cos_twist, sin_twist = turns(np.arange(16), np.arange(128), NX)
    twist = np.stack([cos_twist, sin_twist]).astype(np.float32)
    return np.stack([high, low]), twist


def split(value):
    high = value.astype(BF16)
    low = (value - high.astype(F32)).astype(BF16)
    return high, low


def dot(left, right):
    return jnp.dot(left, right, preferred_element_type=F32)


def dot_nt(left, right):
    return lax.dot_general(left, right, (((1,), (1,)), ((), ())), preferred_element_type=F32)


def time_kernel(
    place_ref,
    screen_ref,
    x_ref,
    one_ref,
    twist_ref,
    two_ref,
    within_ref,
    earlier_ref,
    out_ref,
    high_ref,
    low_ref,
):
    first_point = place_ref[0] * 8
    cos_twist = twist_ref[0]
    sin_twist = twist_ref[1]
    for p in range(8):
        sample = x_ref[pl.ds(p, 128, stride=8), :]
        square = sample * sample
        fourth_high, fourth_low = split(square * square)
        sums = dot(jnp.concatenate([fourth_high, fourth_low], 1), within_ref[...])
        total_high, total_low = split(sums[:, 128:])
        before = dot(earlier_ref[...], jnp.concatenate([total_high, total_low], 0))
        density = (sums[:, :128] + before) * (ionize_rate / NT)
        strength = 2.0 * screen_ref[first_point + p]
        polarization = (kerr_coeff * square + strength) * sample
        current = density * sample
        signals = jnp.concatenate([sample, polarization, current], 1)
        signal_high, signal_low = split(signals)
        stack = jnp.concatenate([signal_high, signal_low, signal_high], 0)
        first = dot(one_ref[...], stack)
        for s in range(3):
            re = first[:128, s * 128 : (s + 1) * 128]
            im = first[128:, s * 128 : (s + 1) * 128]
            turned = jnp.concatenate(
                [re * cos_twist + im * sin_twist, im * cos_twist - re * sin_twist], 1
            )
            high, low = split(turned)
            for c in range(4):
                rows = pl.ds((c * 8 + p) * 32, 32)
                high_ref[s, rows, :] = high[c * 32 : (c + 1) * 32]
                low_ref[s, rows, :] = low[c * 32 : (c + 1) * 32]
    k2 = lax.broadcasted_iota(jnp.int32, (64, 128), 0)
    lane = lax.broadcasted_iota(jnp.int32, (64, 128), 1)
    for c in range(4):
        rows = pl.ds(c * 256, 256)
        parts = []
        for s in range(3):
            both = dot_nt(two_ref[...], high_ref[s, rows, :])
            rest = dot_nt(two_ref[:128], low_ref[s, rows, :])
            value = both[:128] + both[128:] + rest
            parts.append((value[:64], value[64:]))
        scaled = (k2 * 128 + c * 32 + lane % 32).astype(F32) / NF
        kerr = 0.2 * scaled
        plasma = 0.5 / (1.0 + 64.0 * scaled * scaled)
        for h in range(2):
            cut = slice(h * 128, (h + 1) * 128)
            (base_re, base_im), (kerr_re, kerr_im), (plasma_re, plasma_im) = [
                (re[:, cut], im[:, cut]) for re, im in parts
            ]
            mixed_re = base_re - kerr * kerr_im - plasma * plasma_re
            mixed_im = base_im + kerr * kerr_re - plasma * plasma_im
            out_ref[pl.ds(c * 4 + h, 64, stride=16), :] = mixed_re
            out_ref[pl.ds(c * 4 + 2 + h, 64, stride=16), :] = mixed_im


def fft4(values):
    (ar, ai), (br, bi), (cr, ci), (dr, di) = values
    sr, si, tr, ti = ar + cr, ai + ci, ar - cr, ai - ci
    ur, ui, vr, vi = br + dr, bi + di, br - dr, bi - di
    return [(sr + ur, si + ui), (tr + vi, ti - vr), (sr - ur, si - ui), (tr - vi, ti + vr)]


def fft16(values):
    columns = []
    for n in range(4):
        column = fft4([values[4 * m + n] for m in range(4)])
        turned = []
        for k, (re, im) in enumerate(column):
            step = n * k
            if step == 0:
                turned.append((re, im))
            elif step == 4:
                turned.append((im, -re))
            else:
                c = math.cos(2 * math.pi * step / 16)
                s = math.sin(2 * math.pi * step / 16)
                turned.append((re * c + im * s, im * c - re * s))
        columns.append(turned)
    result = [None] * 16
    for k in range(4):
        for m, value in enumerate(fft4([columns[n][k] for n in range(4)])):
            result[k + 4 * m] = value
    return result


def cos_sin(angle):
    quarter = jnp.round(angle * (2.0 / math.pi))
    rest = angle - quarter * 1.5703125
    rest = rest - quarter * 4.837512969970703125e-4
    rest = rest - quarter * 7.54978995489188216e-8
    square = rest * rest
    sine = rest + rest * square * (
        -1.6666654611e-1 + square * (8.3321608736e-3 + square * -1.9515295891e-4)
    )
    cosine = (
        1.0
        - 0.5 * square
        + square
        * square
        * (4.166664568298827e-2 + square * (-1.388731625493765e-3 + square * 2.443315711809948e-5))
    )
    which = quarter.astype(jnp.int32) & 3
    odd = (which & 1) == 1
    cos_out = jnp.where(odd, sine, cosine)
    sin_out = jnp.where(odd, cosine, sine)
    cos_out = jnp.where((which == 1) | (which == 2), -cos_out, cos_out)
    sin_out = jnp.where(which >= 2, -sin_out, sin_out)
    return cos_out, sin_out


def cross_kernel(place_ref, x_ref, table_ref, twist_ref, out_ref, hold_ref):
    grids = []
    for part in range(2):
        columns = []
        for odd in range(2):
            for h in range(2):
                j = part * 2 + h
                pieces = [
                    x_ref[pl.ds((2 * pair + odd) * 128 + j, 32, stride=4), :] for pair in range(4)
                ]
                columns.append(jnp.concatenate(pieces, 0).T)
        grids.append(jnp.concatenate(columns, 0))
    high, low = split(jnp.concatenate(grids, 1))
    hold_ref[...] = dot(high, table_ref[0]) + dot(low, table_ref[0]) + dot(high, table_ref[1])
    first_bin = (place_ref[0] * 32 + place_ref[1]) * 32
    bins = lax.broadcasted_iota(jnp.int32, (8, 128), 0)
    lane = lax.broadcasted_iota(jnp.int32, (8, 128), 1)
    for tile in range(4):
        values = []
        for n in range(16):
            rows = pl.ds(n * 32 + tile * 8, 8)
            re = hold_ref[rows, :128]
            im = hold_ref[rows, 128:]
            c = twist_ref[0, n : n + 1, :]
            s = twist_ref[1, n : n + 1, :]
            values.append((re * c + im * s, im * c - re * s))
        scaled = (first_bin + tile * 8 + bins).astype(F32) / NF
        forward = 40.0 * scaled * (1.0 + 0.3 * scaled * scaled)
        for m, (re, im) in enumerate(fft16(values)):
            q = lane + m * 128
            transverse = jnp.where(q < NX // 2, q, q - NX).astype(F32) / (NX // 2)
            angle = forward - 20.0 * transverse * transverse / (scaled + 0.05)
            c, s = cos_sin(angle)
            out_ref[0, pl.ds(tile * 8, 8), m * 128 : (m + 1) * 128] = re * c - im * s
            out_ref[1, pl.ds(tile * 8, 8), m * 128 : (m + 1) * 128] = re * s + im * c


def time_part(place, screen, samples):
    tables = time_tables()
    in_vmem = pl.BlockSpec(memory_space=pltpu.VMEM)
    in_smem = pl.BlockSpec(memory_space=pltpu.SMEM)
    return pl.pallas_call(
        time_kernel,
        out_shape=jax.ShapeDtypeStruct((1024, 128), F32),
        in_specs=[in_smem, in_smem] + [in_vmem] * 6,
        out_specs=in_vmem,
        scratch_shapes=[pltpu.VMEM((3, 1024, 256), BF16)] * 2,
        compiler_params=pltpu.CompilerParams(vmem_limit_bytes=32 * 2**20),
        name="time_spectra",
    )(place, screen, samples, *tables)


def cross_part(place, blocks):
    tables = cross_tables()
    in_vmem = pl.BlockSpec(memory_space=pltpu.VMEM)
    in_smem = pl.BlockSpec(memory_space=pltpu.SMEM)
    return pl.pallas_call(
        cross_kernel,
        out_shape=jax.ShapeDtypeStruct((2, 32, NX), F32),
        in_specs=[in_smem] + [in_vmem] * 3,
        out_specs=in_vmem,
        scratch_shapes=[pltpu.VMEM((512, 256), F32)],
        compiler_params=pltpu.CompilerParams(vmem_limit_bytes=32 * 2**20),
        name="cross_spectra",
    )(place, blocks, *tables)


def per_device(field, screen):
    place = jnp.stack([lax.axis_index("tm"), lax.axis_index("row")]).astype(jnp.int32)
    mine = field.reshape(8, 8, 16, 128).transpose(0, 2, 1, 3)
    samples = lax.all_to_all(mine, "tm", split_axis=0, concat_axis=0, tiled=True)
    mixed = time_part(place, screen.reshape(64), samples.reshape(1024, 128))
    blocks = lax.all_to_all(
        mixed.reshape(256, 4, 128), ("tm", "row"), split_axis=0, concat_axis=0, tiled=True
    )
    return cross_part(place, blocks.reshape(1024, 128)).reshape(2, 1, 32, NX)


def solution(mesh):
    return jax.shard_map(
        per_device,
        mesh=mesh,
        in_specs=(P(None, "row", "tm"), P(None, "row")),
        out_specs=P(None, None, ("tm", "row"), None),
        check_vma=False,
    )
```

```python
import math

import jax
import jax.numpy as jnp
import ml_dtypes
import numpy as np
from jax import lax
from jax.experimental import pallas as pl
from jax.experimental.pallas import tpu as pltpu
from jax.sharding import PartitionSpec as P

NX = 2048
NT = 16384
NF = 8192

kerr_coeff = 0.3
ionize_rate = 0.4

F32 = jnp.float32
BF16 = jnp.bfloat16


def two_parts(table):
    high = table.astype(ml_dtypes.bfloat16)
    low = (table - high.astype(np.float64)).astype(ml_dtypes.bfloat16)
    return high, low


def turns(left, right, period):
    product = (np.asarray(left)[:, None] * np.asarray(right)[None, :]) % period
    angle = product.astype(np.float64) * (2.0 * math.pi / period)
    return np.cos(angle), np.sin(angle)


def time_tables():
    index = np.arange(128)
    cos_one, sin_one = turns(index, index, 128)
    one_high, one_low = two_parts(np.concatenate([cos_one, -sin_one], 0))
    one = np.concatenate([one_high, one_high, one_low], 1)
    cos_twist, sin_twist = turns(index, index, NT)
    twist = np.stack([cos_twist, sin_twist]).astype(np.float32)
    cos_two, sin_two = turns(np.arange(64), index, 128)
    scale = 1.0 / math.sqrt(NT)
    two = np.block([[cos_two, sin_two], [-sin_two, cos_two]]) * scale
    two_high, two_low = two_parts(two)
    two = np.concatenate([two_high, two_low], 0)
    within = (index[:, None] <= index[None, :]).astype(np.float64)
    within = np.concatenate([within, np.ones((128, 128))], 1)
    within = np.concatenate([within, within], 0).astype(ml_dtypes.bfloat16)
    earlier = (index[None, :] < index[:, None]).astype(np.float64)
    earlier = np.concatenate([earlier, earlier], 1).astype(ml_dtypes.bfloat16)
    return one, twist, two, within, earlier


def cross_tables():
    order = np.arange(128)
    x_hi = (order % 32) * 4 + order // 32
    cos_one, sin_one = turns(x_hi, np.arange(128), 128)
    scale = 1.0 / math.sqrt(NX)
    table = np.block([[cos_one, -sin_one], [sin_one, cos_one]]) * scale
    high, low = two_parts(table)
    cos_twist, sin_twist = turns(np.arange(16), np.arange(128), NX)
    twist = np.stack([cos_twist, sin_twist]).astype(np.float32)
    return np.stack([high, low]), twist


def split(value):
    high = value.astype(BF16)
    low = (value - high.astype(F32)).astype(BF16)
    return high, low


def dot(left, right):
    return jnp.dot(left, right, preferred_element_type=F32)


def dot_nt(left, right):
    return lax.dot_general(left, right, (((1,), (1,)), ((), ())), preferred_element_type=F32)


PAIRS = 2


def time_kernel(
    strength_ref,
    x_ref,
    one_ref,
    twist_ref,
    two_ref,
    within_ref,
    earlier_ref,
    out_ref,
    high_ref,
    low_ref,
    stack_ref,
):
    points = range(8)
    fourths = []
    for p in points:
        sample = x_ref[pl.ds(p, 128, stride=8), :]
        square = sample * sample
        fourths.append(jnp.concatenate(split(square * square), 1))
    sums = dot(jnp.concatenate(fourths, 0), within_ref[...])
    totals = [jnp.concatenate(split(sums[p * 128 : (p + 1) * 128, 128:]), 0) for p in points]
    before = dot(earlier_ref[...], jnp.concatenate(totals, 1))
    for p in points:
        cut = slice(p * 128, (p + 1) * 128)
        sample = x_ref[pl.ds(p, 128, stride=8), :]
        square = sample * sample
        density = (sums[cut, :128] + before[:, cut]) * (ionize_rate / NT)
        polarization = (kerr_coeff * square + strength_ref[p : p + 1, :]) * sample
        current = density * sample
        for s, signal in enumerate((sample, polarization, current)):
            high, low = split(signal)
            lanes = slice((p * 3 + s) * 128, (p * 3 + s + 1) * 128)
            stack_ref[:128, lanes] = high
            stack_ref[128:, lanes] = low
    for pair in range(PAIRS):
        width = 3072 // PAIRS
        lanes = slice(pair * width, (pair + 1) * width)
        first = dot(one_ref[:, :256], stack_ref[:, lanes]) + dot(
            one_ref[:, 256:], stack_ref[:128, lanes]
        )
        for n in range(width // 128):
            p, s = divmod(pair * (width // 128) + n, 3)
            re = first[:128, n * 128 : (n + 1) * 128]
            im = first[128:, n * 128 : (n + 1) * 128]
            cos_twist = twist_ref[0]
            sin_twist = twist_ref[1]
            turned = jnp.concatenate(
                [re * cos_twist + im * sin_twist, im * cos_twist - re * sin_twist], 1
            )
            high, low = split(turned)
            for c in range(4):
                rows = pl.ds((c * 8 + p) * 32, 32)
                high_ref[s, rows, :] = high[c * 32 : (c + 1) * 32]
                low_ref[s, rows, :] = low[c * 32 : (c + 1) * 32]
    k2 = lax.broadcasted_iota(jnp.int32, (64, 128), 0)
    lane = lax.broadcasted_iota(jnp.int32, (64, 128), 1)
    for c in range(4):
        rows = pl.ds(c * 256, 256)
        parts = []
        for s in range(3):
            both = dot_nt(two_ref[...], high_ref[s, rows, :])
            rest = dot_nt(two_ref[:128], low_ref[s, rows, :])
            value = both[:128] + both[128:] + rest
            parts.append((value[:64], value[64:]))
        scaled = (k2 * 128 + c * 32 + lane % 32).astype(F32) / NF
        kerr = 0.2 * scaled
        plasma = 0.5 / (1.0 + 64.0 * scaled * scaled)
        for h in range(2):
            cut = slice(h * 128, (h + 1) * 128)
            (base_re, base_im), (kerr_re, kerr_im), (plasma_re, plasma_im) = [
                (re[:, cut], im[:, cut]) for re, im in parts
            ]
            mixed_re = base_re - kerr * kerr_im - plasma * plasma_re
            mixed_im = base_im + kerr * kerr_re - plasma * plasma_im
            out_ref[pl.ds(c * 4 + h, 64, stride=16), :] = mixed_re
            out_ref[pl.ds(c * 4 + 2 + h, 64, stride=16), :] = mixed_im


def fft4(values):
    (ar, ai), (br, bi), (cr, ci), (dr, di) = values
    sr, si, tr, ti = ar + cr, ai + ci, ar - cr, ai - ci
    ur, ui, vr, vi = br + dr, bi + di, br - dr, bi - di
    return [(sr + ur, si + ui), (tr + vi, ti - vr), (sr - ur, si - ui), (tr - vi, ti + vr)]


def fft16(values):
    columns = []
    for n in range(4):
        column = fft4([values[4 * m + n] for m in range(4)])
        turned = []
        for k, (re, im) in enumerate(column):
            step = n * k
            if step == 0:
                turned.append((re, im))
            elif step == 4:
                turned.append((im, -re))
            else:
                c = math.cos(2 * math.pi * step / 16)
                s = math.sin(2 * math.pi * step / 16)
                turned.append((re * c + im * s, im * c - re * s))
        columns.append(turned)
    result = [None] * 16
    for k in range(4):
        for m, value in enumerate(fft4([columns[n][k] for n in range(4)])):
            result[k + 4 * m] = value
    return result


def cos_sin(angle):
    quarter = jnp.round(angle * (2.0 / math.pi))
    rest = angle - quarter * 1.5703125
    rest = rest - quarter * 4.837512969970703125e-4
    rest = rest - quarter * 7.54978995489188216e-8
    square = rest * rest
    sine = rest + rest * square * (
        -1.6666654611e-1 + square * (8.3321608736e-3 + square * -1.9515295891e-4)
    )
    cosine = (
        1.0
        - 0.5 * square
        + square
        * square
        * (4.166664568298827e-2 + square * (-1.388731625493765e-3 + square * 2.443315711809948e-5))
    )
    which = quarter.astype(jnp.int32) & 3
    odd = (which & 1) == 1
    cos_out = jnp.where(odd, sine, cosine)
    sin_out = jnp.where(odd, cosine, sine)
    cos_out = jnp.where((which == 1) | (which == 2), -cos_out, cos_out)
    sin_out = jnp.where(which >= 2, -sin_out, sin_out)
    return cos_out, sin_out


def cross_kernel(x_ref, table_ref, twist_ref, out_ref, hold_ref, done_ref, sem):
    grids = []
    for part in range(2):
        columns = []
        for odd in range(2):
            for h in range(2):
                j = part * 2 + h
                pieces = [
                    x_ref[pl.ds((2 * pair + odd) * 128 + j, 32, stride=4), :] for pair in range(4)
                ]
                columns.append(jnp.concatenate(pieces, 0))
        grids.append(jnp.concatenate(columns, 1))
    high, low = split(jnp.concatenate(grids, 0))
    high, low = high.T, low.T
    hold_ref[...] = dot(high, table_ref[0]) + dot(low, table_ref[0]) + dot(high, table_ref[1])
    first_bin = lax.axis_index(("tm", "row")) * 32
    bins = lax.broadcasted_iota(jnp.int32, (8, 128), 0)
    lane = lax.broadcasted_iota(jnp.int32, (8, 128), 1)
    copies = []
    for tile in range(4):
        values = []
        for n in range(16):
            rows = pl.ds(n * 32 + tile * 8, 8)
            re = hold_ref[rows, :128]
            im = hold_ref[rows, 128:]
            c = twist_ref[0, n : n + 1, :]
            s = twist_ref[1, n : n + 1, :]
            values.append((re * c + im * s, im * c - re * s))
        scaled = (first_bin + tile * 8 + bins).astype(F32) / NF
        forward = 40.0 * scaled * (1.0 + 0.3 * scaled * scaled)
        for m, (re, im) in enumerate(fft16(values)):
            q = lane + m * 128
            transverse = jnp.where(q < NX // 2, q, q - NX).astype(F32) / (NX // 2)
            angle = forward - 20.0 * transverse * transverse / (scaled + 0.05)
            c, s = cos_sin(angle)
            done_ref[0, pl.ds(tile * 8, 8), m * 128 : (m + 1) * 128] = re * c - im * s
            done_ref[1, pl.ds(tile * 8, 8), m * 128 : (m + 1) * 128] = re * s + im * c
        rows = pl.ds(tile * 8, 8)
        copy = pltpu.make_async_copy(done_ref.at[:, rows], out_ref.at[:, rows], sem.at[tile])
        copy.start()
        copies.append(copy)
    for copy in copies:
        copy.wait()


def time_part(strength, samples):
    tables = time_tables()
    in_vmem = pl.BlockSpec(memory_space=pltpu.VMEM)
    return pl.pallas_call(
        time_kernel,
        out_shape=jax.ShapeDtypeStruct((1024, 128), F32),
        in_specs=[in_vmem] * 7,
        out_specs=in_vmem,
        scratch_shapes=[pltpu.VMEM((3, 1024, 256), BF16)] * 2 + [pltpu.VMEM((256, 3072), BF16)],
        compiler_params=pltpu.CompilerParams(vmem_limit_bytes=32 * 2**20),
        name="time_spectra",
    )(strength, samples, *tables)


def cross_part(blocks):
    tables = cross_tables()
    in_vmem = pl.BlockSpec(memory_space=pltpu.VMEM)
    return pl.pallas_call(
        cross_kernel,
        out_shape=jax.ShapeDtypeStruct((2, 32, NX), F32),
        in_specs=[in_vmem] * 3,
        out_specs=pl.BlockSpec(memory_space=pl.ANY),
        scratch_shapes=[
            pltpu.VMEM((512, 256), F32),
            pltpu.VMEM((2, 32, NX), F32),
            pltpu.SemaphoreType.DMA((4,)),
        ],
        compiler_params=pltpu.CompilerParams(vmem_limit_bytes=32 * 2**20),
        name="cross_spectra",
    )(blocks, *tables)


def per_device(field, screen):
    mine = field.reshape(8, 8, 16, 128).transpose(0, 2, 1, 3)
    samples = lax.all_to_all(mine, "tm", split_axis=0, concat_axis=0, tiled=True)
    strength = 2.0 * lax.dynamic_slice_in_dim(screen.reshape(64, 1), lax.axis_index("tm") * 8, 8)
    mixed = time_part(jnp.broadcast_to(strength, (8, 128)), samples.reshape(1024, 128))
    blocks = lax.all_to_all(
        mixed.reshape(256, 4, 128), ("tm", "row"), split_axis=0, concat_axis=0, tiled=True
    )
    return cross_part(blocks.reshape(1024, 128)).reshape(2, 1, 32, NX)


def solution(mesh):
    return jax.shard_map(
        per_device,
        mesh=mesh,
        in_specs=(P(None, "row", "tm"), P(None, "row")),
        out_specs=P(None, None, ("tm", "row"), None),
        check_vma=False,
    )
```

```python
import math

import jax
import jax.numpy as jnp
import ml_dtypes
import numpy as np
from jax import lax
from jax.experimental import pallas as pl
from jax.experimental.pallas import tpu as pltpu
from jax.sharding import PartitionSpec as P

NX = 2048
NT = 16384
NF = 8192

kerr_coeff = 0.3
ionize_rate = 0.4

F32 = jnp.float32
BF16 = jnp.bfloat16


def two_parts(table):
    high = table.astype(ml_dtypes.bfloat16)
    low = (table - high.astype(np.float64)).astype(ml_dtypes.bfloat16)
    return high, low


def turns(left, right, period):
    product = (np.asarray(left)[:, None] * np.asarray(right)[None, :]) % period
    angle = product.astype(np.float64) * (2.0 * math.pi / period)
    return np.cos(angle), np.sin(angle)


def time_tables():
    index = np.arange(128)
    cos_one, sin_one = turns(index, index, 128)
    one_high, one_low = two_parts(np.concatenate([cos_one, -sin_one], 0))
    one = np.concatenate([one_high, one_high, one_low], 1)
    cos_twist, sin_twist = turns(index, index, NT)
    twist = np.stack([cos_twist, sin_twist]).astype(np.float32)
    cos_two, sin_two = turns(np.arange(64), index, 128)
    scale = 1.0 / math.sqrt(NT)
    two = np.block([[cos_two, sin_two], [-sin_two, cos_two]]) * scale
    two_high, two_low = two_parts(two)
    two = np.concatenate([two_high, two_low], 0)
    within = (index[:, None] <= index[None, :]).astype(np.float64)
    within = np.concatenate([within, np.ones((128, 128))], 1)
    within = np.concatenate([within, within], 0).astype(ml_dtypes.bfloat16)
    earlier = (index[None, :] < index[:, None]).astype(np.float64)
    earlier = np.concatenate([earlier, earlier], 1).astype(ml_dtypes.bfloat16)
    return one, twist, two, within, earlier


def cross_tables():
    order = np.arange(128)
    x_hi = (order % 32) * 4 + order // 32
    cos_one, sin_one = turns(x_hi, np.arange(128), 128)
    scale = 1.0 / math.sqrt(NX)
    table = np.block([[cos_one, -sin_one], [sin_one, cos_one]]) * scale
    high, low = two_parts(table)
    cos_twist, sin_twist = turns(np.arange(16), np.arange(128), NX)
    twist = np.stack([cos_twist, sin_twist]).astype(np.float32)
    return np.stack([high, low]), twist


def split(value):
    high = value.astype(BF16)
    low = (value - high.astype(F32)).astype(BF16)
    return high, low


def dot(left, right):
    return jnp.dot(left, right, preferred_element_type=F32)


def dot_nt(left, right):
    return lax.dot_general(left, right, (((1,), (1,)), ((), ())), preferred_element_type=F32)


PAIRS = 2


def time_kernel(
    strength_ref,
    x_ref,
    one_ref,
    twist_ref,
    two_ref,
    within_ref,
    earlier_ref,
    out_ref,
    high_ref,
    low_ref,
    stack_ref,
):
    points = range(8)
    fourths = []
    for p in points:
        sample = x_ref[pl.ds(p, 128, stride=8), :]
        square = sample * sample
        fourths.append(jnp.concatenate(split(square * square), 1))
    sums = dot(jnp.concatenate(fourths, 0), within_ref[...])
    totals = [jnp.concatenate(split(sums[p * 128 : (p + 1) * 128, 128:]), 0) for p in points]
    before = dot(earlier_ref[...], jnp.concatenate(totals, 1))
    for p in points:
        cut = slice(p * 128, (p + 1) * 128)
        sample = x_ref[pl.ds(p, 128, stride=8), :]
        square = sample * sample
        density = (sums[cut, :128] + before[:, cut]) * (ionize_rate / NT)
        polarization = (kerr_coeff * square + strength_ref[p : p + 1, :]) * sample
        current = density * sample
        for s, signal in enumerate((sample, polarization, current)):
            high, low = split(signal)
            lanes = slice((p * 3 + s) * 128, (p * 3 + s + 1) * 128)
            stack_ref[:128, lanes] = high
            stack_ref[128:, lanes] = low
    for pair in range(PAIRS):
        width = 3072 // PAIRS
        lanes = slice(pair * width, (pair + 1) * width)
        first = dot(one_ref[:, :256], stack_ref[:, lanes]) + dot(
            one_ref[:, 256:], stack_ref[:128, lanes]
        )
        for n in range(width // 128):
            p, s = divmod(pair * (width // 128) + n, 3)
            re = first[:128, n * 128 : (n + 1) * 128]
            im = first[128:, n * 128 : (n + 1) * 128]
            cos_twist = twist_ref[0]
            sin_twist = twist_ref[1]
            turned = jnp.concatenate(
                [re * cos_twist + im * sin_twist, im * cos_twist - re * sin_twist], 1
            )
            high, low = split(turned)
            for c in range(4):
                rows = pl.ds((c * 8 + p) * 32, 32)
                high_ref[s, rows, :] = high[c * 32 : (c + 1) * 32]
                low_ref[s, rows, :] = low[c * 32 : (c + 1) * 32]
    k2 = lax.broadcasted_iota(jnp.int32, (64, 128), 0)
    lane = lax.broadcasted_iota(jnp.int32, (64, 128), 1)
    for c in range(4):
        rows = pl.ds(c * 256, 256)
        parts = []
        for s in range(3):
            both = dot_nt(two_ref[...], high_ref[s, rows, :])
            rest = dot_nt(two_ref[:128], low_ref[s, rows, :])
            value = both[:128] + both[128:] + rest
            parts.append((value[:64], value[64:]))
        scaled = (k2 * 128 + c * 32 + lane % 32).astype(F32) / NF
        kerr = 0.2 * scaled
        plasma = 0.5 / (1.0 + 64.0 * scaled * scaled)
        for h in range(2):
            cut = slice(h * 128, (h + 1) * 128)
            (base_re, base_im), (kerr_re, kerr_im), (plasma_re, plasma_im) = [
                (re[:, cut], im[:, cut]) for re, im in parts
            ]
            mixed_re = base_re - kerr * kerr_im - plasma * plasma_re
            mixed_im = base_im + kerr * kerr_re - plasma * plasma_im
            out_ref[pl.ds(c * 4 + h, 64, stride=16), :] = mixed_re
            out_ref[pl.ds(c * 4 + 2 + h, 64, stride=16), :] = mixed_im


def fft4(values):
    (ar, ai), (br, bi), (cr, ci), (dr, di) = values
    sr, si, tr, ti = ar + cr, ai + ci, ar - cr, ai - ci
    ur, ui, vr, vi = br + dr, bi + di, br - dr, bi - di
    return [(sr + ur, si + ui), (tr + vi, ti - vr), (sr - ur, si - ui), (tr - vi, ti + vr)]


def fft16(values):
    columns = []
    for n in range(4):
        column = fft4([values[4 * m + n] for m in range(4)])
        turned = []
        for k, (re, im) in enumerate(column):
            step = n * k
            if step == 0:
                turned.append((re, im))
            elif step == 4:
                turned.append((im, -re))
            else:
                c = math.cos(2 * math.pi * step / 16)
                s = math.sin(2 * math.pi * step / 16)
                turned.append((re * c + im * s, im * c - re * s))
        columns.append(turned)
    result = [None] * 16
    for k in range(4):
        for m, value in enumerate(fft4([columns[n][k] for n in range(4)])):
            result[k + 4 * m] = value
    return result


def cos_sin(angle):
    quarter = jnp.round(angle * (2.0 / math.pi))
    rest = angle - quarter * 1.5703125
    rest = rest - quarter * 4.837512969970703125e-4
    rest = rest - quarter * 7.54978995489188216e-8
    square = rest * rest
    sine = rest + rest * square * (
        -1.6666654611e-1 + square * (8.3321608736e-3 + square * -1.9515295891e-4)
    )
    cosine = (
        1.0
        - 0.5 * square
        + square
        * square
        * (4.166664568298827e-2 + square * (-1.388731625493765e-3 + square * 2.443315711809948e-5))
    )
    which = quarter.astype(jnp.int32) & 3
    odd = (which & 1) == 1
    cos_out = jnp.where(odd, sine, cosine)
    sin_out = jnp.where(odd, cosine, sine)
    cos_out = jnp.where((which == 1) | (which == 2), -cos_out, cos_out)
    sin_out = jnp.where(which >= 2, -sin_out, sin_out)
    return cos_out, sin_out


def prepare_kernel(screen_ref, strength_ref, phase_ref):
    screen = jnp.broadcast_to(jnp.concatenate([screen_ref[...]] * 2, 1), (8, 128))
    first_point = lax.axis_index("tm") * 8
    mine = 2.0 * pltpu.roll(screen, (128 - first_point) % 128, 1)
    for p in range(8):
        strength_ref[p : p + 1, :] = jnp.broadcast_to(mine[:1, p : p + 1], (1, 128))
    first_bin = lax.axis_index(("tm", "row")) * 32
    bins = lax.broadcasted_iota(jnp.int32, (8, 128), 0)
    lane = lax.broadcasted_iota(jnp.int32, (8, 128), 1)
    for tile in range(4):
        scaled = (first_bin + tile * 8 + bins).astype(F32) / NF
        forward = 40.0 * scaled * (1.0 + 0.3 * scaled * scaled)
        for m in range(16):
            q = lane + m * 128
            transverse = jnp.where(q < NX // 2, q, q - NX).astype(F32) / (NX // 2)
            angle = forward - 20.0 * transverse * transverse / (scaled + 0.05)
            for part, value in enumerate(cos_sin(angle)):
                phase_ref[part, pl.ds(tile * 8, 8), m * 128 : (m + 1) * 128] = value


def cross_kernel(x_ref, phase_ref, table_ref, twist_ref, out_ref, done_ref, sem):
    blocks = []
    for part in range(2):
        for odd in range(2):
            for h in range(2):
                j = part * 2 + h
                pieces = [
                    x_ref[pl.ds((2 * pair + odd) * 128 + j, 32, stride=4), :] for pair in range(4)
                ]
                blocks.append(jnp.concatenate(pieces, 0).T)
    copies = []
    for tile in range(4):
        rows = [slice(n * 32 + tile * 8, n * 32 + tile * 8 + 8) for n in range(4)]
        grid = jnp.concatenate(
            [
                jnp.concatenate([blocks[part * 4 + n // 4][rows[n % 4]] for n in range(16)], 0)
                for part in range(2)
            ],
            1,
        )
        high, low = split(grid)
        first = dot(high, table_ref[0]) + dot(low, table_ref[0]) + dot(high, table_ref[1])
        values = []
        for n in range(16):
            re = first[n * 8 : n * 8 + 8, :128]
            im = first[n * 8 : n * 8 + 8, 128:]
            c = twist_ref[0, n : n + 1, :]
            s = twist_ref[1, n : n + 1, :]
            values.append((re * c + im * s, im * c - re * s))
        rows = pl.ds(tile * 8, 8)
        for m, (re, im) in enumerate(fft16(values)):
            lanes = slice(m * 128, (m + 1) * 128)
            c = phase_ref[0, rows, lanes]
            s = phase_ref[1, rows, lanes]
            done_ref[0, rows, lanes] = re * c - im * s
            done_ref[1, rows, lanes] = re * s + im * c
        copy = pltpu.make_async_copy(done_ref.at[:, rows], out_ref.at[:, rows], sem.at[tile])
        copy.start()
        copies.append(copy)
    for copy in copies:
        copy.wait()


def prepare_part(screen):
    in_vmem = pl.BlockSpec(memory_space=pltpu.VMEM)
    return pl.pallas_call(
        prepare_kernel,
        out_shape=[
            jax.ShapeDtypeStruct((8, 128), F32),
            jax.ShapeDtypeStruct((2, 32, NX), F32),
        ],
        in_specs=[in_vmem],
        out_specs=[in_vmem, in_vmem],
        cost_estimate=pl.CostEstimate(flops=4000000, bytes_accessed=524288, transcendentals=0),
        compiler_params=pltpu.CompilerParams(vmem_limit_bytes=16 * 2**20),
        name="prepare",
    )(screen)


def time_part(strength, samples):
    tables = time_tables()
    in_vmem = pl.BlockSpec(memory_space=pltpu.VMEM)
    return pl.pallas_call(
        time_kernel,
        out_shape=jax.ShapeDtypeStruct((1024, 128), F32),
        in_specs=[in_vmem] * 7,
        out_specs=in_vmem,
        scratch_shapes=[pltpu.VMEM((3, 1024, 256), BF16)] * 2 + [pltpu.VMEM((256, 3072), BF16)],
        compiler_params=pltpu.CompilerParams(vmem_limit_bytes=32 * 2**20),
        name="time_spectra",
    )(strength, samples, *tables)


def cross_part(blocks, phases):
    tables = cross_tables()
    in_vmem = pl.BlockSpec(memory_space=pltpu.VMEM)
    return pl.pallas_call(
        cross_kernel,
        out_shape=jax.ShapeDtypeStruct((2, 32, NX), F32),
        in_specs=[in_vmem] * 4,
        out_specs=pl.BlockSpec(memory_space=pl.ANY),
        scratch_shapes=[
            pltpu.VMEM((2, 32, NX), F32),
            pltpu.SemaphoreType.DMA((4,)),
        ],
        compiler_params=pltpu.CompilerParams(vmem_limit_bytes=32 * 2**20),
        name="cross_spectra",
    )(blocks, phases, *tables)


def per_device(field, screen):
    mine = field.reshape(8, 8, 16, 128).transpose(0, 2, 1, 3)
    samples = lax.all_to_all(mine, "tm", split_axis=0, concat_axis=0, tiled=True)
    strength, phases = prepare_part(screen)
    mixed = time_part(strength, samples.reshape(1024, 128))
    blocks = lax.all_to_all(
        mixed.reshape(256, 4, 128), ("tm", "row"), split_axis=0, concat_axis=0, tiled=True
    )
    return cross_part(blocks.reshape(1024, 128), phases).reshape(2, 1, 32, NX)


def solution(mesh):
    return jax.shard_map(
        per_device,
        mesh=mesh,
        in_specs=(P(None, "row", "tm"), P(None, "row")),
        out_specs=P(None, None, ("tm", "row"), None),
        check_vma=False,
    )
```

```python
import math

import jax
import jax.numpy as jnp
import ml_dtypes
import numpy as np
from jax import lax
from jax.experimental import pallas as pl
from jax.experimental.pallas import tpu as pltpu
from jax.sharding import PartitionSpec as P

NX = 2048
NT = 16384
NF = 8192

kerr_coeff = 0.3
ionize_rate = 0.4

F32 = jnp.float32
BF16 = jnp.bfloat16


def two_parts(table):
    high = table.astype(ml_dtypes.bfloat16)
    low = (table - high.astype(np.float64)).astype(ml_dtypes.bfloat16)
    return high, low


def turns(left, right, period):
    product = (np.asarray(left)[:, None] * np.asarray(right)[None, :]) % period
    angle = product.astype(np.float64) * (2.0 * math.pi / period)
    return np.cos(angle), np.sin(angle)


def time_tables():
    index = np.arange(128)
    cos_one, sin_one = turns(index, index, 128)
    one_high, one_low = two_parts(np.concatenate([cos_one, -sin_one], 1))
    one = np.concatenate([one_high, one_high, one_low], 0)
    cos_twist, sin_twist = turns(index, index, NT)
    twist = np.stack([cos_twist, sin_twist]).astype(np.float32)
    cos_two, sin_two = turns(np.arange(64), index, 128)
    scale = 1.0 / math.sqrt(NT)
    two = np.concatenate(
        two_parts(np.block([[cos_two, sin_two], [-sin_two, cos_two]]) * scale), 0
    )
    within = (index[None, :] <= index[:, None]).astype(np.float64)
    within = np.concatenate([within, np.ones((16, 128))], 0)
    within = np.concatenate([within, within], 1).astype(ml_dtypes.bfloat16)
    earlier = (index[:, None] < index[None, :]).astype(np.float64)
    earlier = np.concatenate([earlier, earlier], 0).astype(ml_dtypes.bfloat16)
    return one, twist, two, within, earlier


def cross_tables():
    order = np.arange(128)
    x_hi = (order % 32) * 4 + order // 32
    cos_one, sin_one = turns(x_hi, np.arange(128), 128)
    scale = 1.0 / math.sqrt(NX)
    table = np.block([[cos_one, -sin_one], [sin_one, cos_one]]) * scale
    high, low = two_parts(table)
    cos_twist, sin_twist = turns(np.arange(16), np.arange(128), NX)
    twist = np.stack([cos_twist, sin_twist]).astype(np.float32)
    return np.stack([high, low]), twist


def split(value):
    high = value.astype(BF16)
    low = (value - high.astype(F32)).astype(BF16)
    return high, low


def dot(left, right):
    return jnp.dot(left, right, preferred_element_type=F32)


def exchange_blocks(values):
    lane = lax.broadcasted_iota(jnp.int32, values[0].shape, 1)
    for width in (32, 64):
        low = (lane & width) == 0
        step = width // 32
        result = [None] * 4
        for n in range(4):
            if n & step == 0:
                first, second = values[n], values[n + step]
                result[n] = jnp.where(low, first, pltpu.roll(second, width, 1))
                result[n + step] = jnp.where(low, pltpu.roll(first, 128 - width, 1), second)
        values = result
    return values


def time_kernel(
    strength_ref,
    x_ref,
    one_ref,
    twist_ref,
    two_ref,
    within_ref,
    earlier_ref,
    out_ref,
    turned_ref,
    high_ref,
    low_ref,
):
    points = range(8)
    cuts = [slice(p * 128, (p + 1) * 128) for p in points]
    fourths = []
    for p in points:
        sample = x_ref[pl.ds(p, 128, stride=8), :].T
        turned_ref[cuts[p], :] = sample
        square = sample * sample
        fourths.append(jnp.concatenate(split(square * square), 0))
    sums = dot(within_ref[...], jnp.concatenate(fourths, 1))
    totals = [jnp.concatenate(split(sums[128:, cut]), 1) for cut in cuts]
    before = dot(jnp.concatenate(totals, 0), earlier_ref[...])
    for group in range(8 // GROUP):
        rows = []
        for p in range(group * GROUP, (group + 1) * GROUP):
            sample = turned_ref[cuts[p], :]
            density = (sums[:128, cuts[p]] + before[p * 16 : p * 16 + 1]) * (ionize_rate / NT)
            polarization = (kerr_coeff * sample * sample + strength_ref[p : p + 1, :]) * sample
            current = density * sample
            for signal in (sample, polarization, current):
                rows.append(jnp.concatenate(split(signal), 1))
        rows = jnp.concatenate(rows, 0)
        first = dot(rows, one_ref[:256]) + dot(rows[:, :128], one_ref[256:])
        for n in range(GROUP * 3):
            p, s = divmod(group * GROUP * 3 + n, 3)
            re = first[n * 128 : (n + 1) * 128, :128]
            im = first[n * 128 : (n + 1) * 128, 128:]
            cos_twist = twist_ref[0]
            sin_twist = twist_ref[1]
            lanes = slice((s * 8 + p) * 128, (s * 8 + p + 1) * 128)
            for part, value in enumerate(
                (re * cos_twist + im * sin_twist, im * cos_twist - re * sin_twist)
            ):
                high, low = split(value)
                high_ref[part * 128 : (part + 1) * 128, lanes] = high
                low_ref[part * 128 : (part + 1) * 128, lanes] = low
    k2 = lax.broadcasted_iota(jnp.int32, (64, 128), 0)
    lane = lax.broadcasted_iota(jnp.int32, (64, 128), 1)
    scaled = (k2 * 128 + lane).astype(F32) / NF
    kerr = 0.2 * scaled
    plasma = 0.5 / (1.0 + 64.0 * scaled * scaled)
    for h in range(2):
        mixed = [[], []]
        for pair in range(2):
            parts = []
            for s in range(3):
                lanes = slice((s * 8 + h * 4 + pair * 2) * 128, (s * 8 + h * 4 + pair * 2 + 2) * 128)
                both = dot(two_ref[...], high_ref[:, lanes])
                rest = dot(two_ref[:128], low_ref[:, lanes])
                parts.append(both[:128] + both[128:] + rest)
            for n in range(2):
                (base_re, base_im), (kerr_re, kerr_im), (plasma_re, plasma_im) = [
                    (part[:64, cuts[n]], part[64:, cuts[n]]) for part in parts
                ]
                mixed[0].append(base_re - kerr * kerr_im - plasma * plasma_re)
                mixed[1].append(base_im + kerr * kerr_re - plasma * plasma_im)
        for part in range(2):
            for c, value in enumerate(exchange_blocks(mixed[part])):
                out_ref[pl.ds(c * 4 + part * 2 + h, 64, stride=16), :] = value


GROUP = 1


def fft4(values):
    (ar, ai), (br, bi), (cr, ci), (dr, di) = values
    sr, si, tr, ti = ar + cr, ai + ci, ar - cr, ai - ci
    ur, ui, vr, vi = br + dr, bi + di, br - dr, bi - di
    return [(sr + ur, si + ui), (tr + vi, ti - vr), (sr - ur, si - ui), (tr - vi, ti + vr)]


def fft16(values):
    columns = []
    for n in range(4):
        column = fft4([values[4 * m + n] for m in range(4)])
        turned = []
        for k, (re, im) in enumerate(column):
            step = n * k
            if step == 0:
                turned.append((re, im))
            elif step == 4:
                turned.append((im, -re))
            else:
                c = math.cos(2 * math.pi * step / 16)
                s = math.sin(2 * math.pi * step / 16)
                turned.append((re * c + im * s, im * c - re * s))
        columns.append(turned)
    result = [None] * 16
    for k in range(4):
        for m, value in enumerate(fft4([columns[n][k] for n in range(4)])):
            result[k + 4 * m] = value
    return result


def cos_sin(angle):
    quarter = jnp.round(angle * (2.0 / math.pi))
    rest = angle - quarter * 1.5703125
    rest = rest - quarter * 4.837512969970703125e-4
    rest = rest - quarter * 7.54978995489188216e-8
    square = rest * rest
    sine = rest + rest * square * (
        -1.6666654611e-1 + square * (8.3321608736e-3 + square * -1.9515295891e-4)
    )
    cosine = (
        1.0
        - 0.5 * square
        + square
        * square
        * (4.166664568298827e-2 + square * (-1.388731625493765e-3 + square * 2.443315711809948e-5))
    )
    which = quarter.astype(jnp.int32) & 3
    odd = (which & 1) == 1
    cos_out = jnp.where(odd, sine, cosine)
    sin_out = jnp.where(odd, cosine, sine)
    cos_out = jnp.where((which == 1) | (which == 2), -cos_out, cos_out)
    sin_out = jnp.where(which >= 2, -sin_out, sin_out)
    return cos_out, sin_out


def prepare_kernel(screen_ref, strength_ref, phase_ref):
    screen = jnp.broadcast_to(jnp.concatenate([screen_ref[...]] * 2, 1), (8, 128))
    first_point = lax.axis_index("tm") * 8
    mine = 2.0 * pltpu.roll(screen, (128 - first_point) % 128, 1)
    for p in range(8):
        strength_ref[p : p + 1, :] = jnp.broadcast_to(mine[:1, p : p + 1], (1, 128))
    first_bin = lax.axis_index(("tm", "row")) * 32
    bins = lax.broadcasted_iota(jnp.int32, (8, 128), 0)
    lane = lax.broadcasted_iota(jnp.int32, (8, 128), 1)
    for tile in range(4):
        scaled = (first_bin + tile * 8 + bins).astype(F32) / NF
        forward = 40.0 * scaled * (1.0 + 0.3 * scaled * scaled)
        for m in range(16):
            q = lane + m * 128
            transverse = jnp.where(q < NX // 2, q, q - NX).astype(F32) / (NX // 2)
            angle = forward - 20.0 * transverse * transverse / (scaled + 0.05)
            for part, value in enumerate(cos_sin(angle)):
                phase_ref[part, pl.ds(tile * 8, 8), m * 128 : (m + 1) * 128] = value


def cross_kernel(x_ref, phase_ref, table_ref, twist_ref, out_ref, done_ref, sem):
    blocks = []
    for part in range(2):
        for odd in range(2):
            for h in range(2):
                j = part * 2 + h
                pieces = [
                    x_ref[pl.ds((2 * pair + odd) * 128 + j, 32, stride=4), :] for pair in range(4)
                ]
                blocks.append(jnp.concatenate(pieces, 0).T)
    copies = []
    for tile in range(4):
        rows = [slice(n * 32 + tile * 8, n * 32 + tile * 8 + 8) for n in range(4)]
        grid = jnp.concatenate(
            [
                jnp.concatenate([blocks[part * 4 + n // 4][rows[n % 4]] for n in range(16)], 0)
                for part in range(2)
            ],
            1,
        )
        high, low = split(grid)
        first = dot(high, table_ref[0]) + dot(low, table_ref[0]) + dot(high, table_ref[1])
        values = []
        for n in range(16):
            re = first[n * 8 : n * 8 + 8, :128]
            im = first[n * 8 : n * 8 + 8, 128:]
            c = twist_ref[0, n : n + 1, :]
            s = twist_ref[1, n : n + 1, :]
            values.append((re * c + im * s, im * c - re * s))
        rows = pl.ds(tile * 8, 8)
        for m, (re, im) in enumerate(fft16(values)):
            lanes = slice(m * 128, (m + 1) * 128)
            c = phase_ref[0, rows, lanes]
            s = phase_ref[1, rows, lanes]
            done_ref[0, rows, lanes] = re * c - im * s
            done_ref[1, rows, lanes] = re * s + im * c
        copy = pltpu.make_async_copy(done_ref.at[:, rows], out_ref.at[:, rows], sem.at[tile])
        copy.start()
        copies.append(copy)
    for copy in copies:
        copy.wait()


def prepare_part(screen):
    in_vmem = pl.BlockSpec(memory_space=pltpu.VMEM)
    return pl.pallas_call(
        prepare_kernel,
        out_shape=[
            jax.ShapeDtypeStruct((8, 128), F32),
            jax.ShapeDtypeStruct((2, 32, NX), F32),
        ],
        in_specs=[in_vmem],
        out_specs=[in_vmem, in_vmem],
        cost_estimate=pl.CostEstimate(flops=4000000, bytes_accessed=524288, transcendentals=0),
        compiler_params=pltpu.CompilerParams(vmem_limit_bytes=16 * 2**20),
        name="prepare",
    )(screen)


def time_part(strength, samples):
    tables = time_tables()
    in_vmem = pl.BlockSpec(memory_space=pltpu.VMEM)
    return pl.pallas_call(
        time_kernel,
        out_shape=jax.ShapeDtypeStruct((1024, 128), F32),
        in_specs=[in_vmem] * 7,
        out_specs=in_vmem,
        scratch_shapes=[pltpu.VMEM((1024, 128), F32)] + [pltpu.VMEM((256, 3072), BF16)] * 2,
        compiler_params=pltpu.CompilerParams(vmem_limit_bytes=32 * 2**20),
        name="time_spectra",
    )(strength, samples, *tables)


def cross_part(blocks, phases):
    tables = cross_tables()
    in_vmem = pl.BlockSpec(memory_space=pltpu.VMEM)
    return pl.pallas_call(
        cross_kernel,
        out_shape=jax.ShapeDtypeStruct((2, 32, NX), F32),
        in_specs=[in_vmem] * 4,
        out_specs=pl.BlockSpec(memory_space=pl.ANY),
        scratch_shapes=[
            pltpu.VMEM((2, 32, NX), F32),
            pltpu.SemaphoreType.DMA((4,)),
        ],
        compiler_params=pltpu.CompilerParams(vmem_limit_bytes=32 * 2**20),
        name="cross_spectra",
    )(blocks, phases, *tables)


def per_device(field, screen):
    mine = field.reshape(8, 8, 16, 128).transpose(0, 2, 1, 3)
    samples = lax.all_to_all(mine, "tm", split_axis=0, concat_axis=0, tiled=True)
    strength, phases = prepare_part(screen)
    mixed = time_part(strength, samples.reshape(1024, 128))
    blocks = lax.all_to_all(
        mixed.reshape(256, 4, 128), ("tm", "row"), split_axis=0, concat_axis=0, tiled=True
    )
    return cross_part(blocks.reshape(1024, 128), phases).reshape(2, 1, 32, NX)


def solution(mesh):
    return jax.shard_map(
        per_device,
        mesh=mesh,
        in_specs=(P(None, "row", "tm"), P(None, "row")),
        out_specs=P(None, None, ("tm", "row"), None),
        check_vma=False,
    )
```

```python
import math

import jax
import jax.numpy as jnp
import ml_dtypes
import numpy as np
from jax import lax
from jax.experimental import pallas as pl
from jax.experimental.pallas import tpu as pltpu
from jax.sharding import PartitionSpec as P

NX = 2048
NT = 16384
NF = 8192

kerr_coeff = 0.3
ionize_rate = 0.4

F32 = jnp.float32
BF16 = jnp.bfloat16


def places():
    place = np.arange(256)
    return place // 32, place // 8 % 4, place // 4 % 2, place // 2 % 2, place % 2


def device_at():
    z, x, y_hi, y_lo, core = places()
    return ((y_hi * 4 + x) * 2 + y_lo) * 16 + z * 2 + core


def two_parts(table):
    high = table.astype(ml_dtypes.bfloat16)
    low = (table - high.astype(np.float64)).astype(ml_dtypes.bfloat16)
    return high, low


def turns(left, right, period):
    product = (np.asarray(left)[:, None] * np.asarray(right)[None, :]) % period
    angle = product.astype(np.float64) * (2.0 * math.pi / period)
    return np.cos(angle), np.sin(angle)


def time_tables():
    index = np.arange(128)
    cos_one, sin_one = turns(index, index, 128)
    one_high, one_low = two_parts(np.concatenate([cos_one, -sin_one], 1))
    one = np.concatenate([one_high, one_high, one_low], 0)
    cos_twist, sin_twist = turns(index, index, NT)
    twist = np.stack([cos_twist, sin_twist]).astype(np.float32)
    cos_two, sin_two = turns(device_at().reshape(4, 2, 16, 2)[:, 0, :, 0].ravel() // 4, index, 128)
    scale = 1.0 / math.sqrt(NT)
    two = np.concatenate(
        two_parts(np.block([[cos_two, sin_two], [-sin_two, cos_two]]) * scale), 0
    )
    within = (index[None, :] <= index[:, None]).astype(np.float64)
    within = np.concatenate([within, np.ones((16, 128))], 0)
    within = np.concatenate([within, within], 1).astype(ml_dtypes.bfloat16)
    earlier = (index[:, None] < index[None, :]).astype(np.float64)
    earlier = np.concatenate([earlier, earlier], 0).astype(ml_dtypes.bfloat16)
    return one, twist, two, within, earlier


def cross_tables():
    even = device_at()[places()[1] % 2 == 0]
    x_hi = (even % 32) * 4 + even // 64
    cos_one, sin_one = turns(x_hi, np.arange(128), 128)
    scale = 1.0 / math.sqrt(NX)
    table = np.block([[cos_one, -sin_one], [sin_one, cos_one]]) * scale
    high, low = two_parts(table)
    cos_twist, sin_twist = turns(np.arange(16), np.arange(128), NX)
    twist = np.stack([cos_twist, sin_twist]).astype(np.float32)
    return np.stack([high, low]), twist


def split(value):
    high = value.astype(BF16)
    low = (value - high.astype(F32)).astype(BF16)
    return high, low


def dot(left, right):
    return jnp.dot(left, right, preferred_element_type=F32)


def exchange_blocks(values):
    lane = lax.broadcasted_iota(jnp.int32, values[0].shape, 1)
    for width in (32, 64):
        low = (lane & width) == 0
        step = width // 32
        result = [None] * 4
        for n in range(4):
            if n & step == 0:
                first, second = values[n], values[n + step]
                result[n] = jnp.where(low, first, pltpu.roll(second, width, 1))
                result[n + step] = jnp.where(low, pltpu.roll(first, 128 - width, 1), second)
        values = result
    return values


def time_kernel(
    strength_ref,
    x_ref,
    one_ref,
    twist_ref,
    two_ref,
    within_ref,
    earlier_ref,
    out_ref,
    turned_ref,
    high_ref,
    low_ref,
):
    points = range(8)
    cuts = [slice(p * 128, (p + 1) * 128) for p in points]
    fourths = []
    for p in points:
        sample = x_ref[pl.ds(p, 128, stride=8), :].T
        turned_ref[cuts[p], :] = sample
        square = sample * sample
        fourths.append(jnp.concatenate(split(square * square), 0))
    sums = dot(within_ref[...], jnp.concatenate(fourths, 1))
    totals = [jnp.concatenate(split(sums[128:, cut]), 1) for cut in cuts]
    before = dot(jnp.concatenate(totals, 0), earlier_ref[...])
    for group in range(8 // GROUP):
        rows = []
        for p in range(group * GROUP, (group + 1) * GROUP):
            sample = turned_ref[cuts[p], :]
            density = (sums[:128, cuts[p]] + before[p * 16 : p * 16 + 1]) * (ionize_rate / NT)
            polarization = (kerr_coeff * sample * sample + strength_ref[p : p + 1, :]) * sample
            current = density * sample
            for signal in (sample, polarization, current):
                rows.append(jnp.concatenate(split(signal), 1))
        rows = jnp.concatenate(rows, 0)
        first = dot(rows, one_ref[:256]) + dot(rows[:, :128], one_ref[256:])
        for n in range(GROUP * 3):
            p, s = divmod(group * GROUP * 3 + n, 3)
            re = first[n * 128 : (n + 1) * 128, :128]
            im = first[n * 128 : (n + 1) * 128, 128:]
            cos_twist = twist_ref[0]
            sin_twist = twist_ref[1]
            lanes = slice((s * 8 + p) * 128, (s * 8 + p + 1) * 128)
            for part, value in enumerate(
                (re * cos_twist + im * sin_twist, im * cos_twist - re * sin_twist)
            ):
                high, low = split(value)
                high_ref[part * 128 : (part + 1) * 128, lanes] = high
                low_ref[part * 128 : (part + 1) * 128, lanes] = low
    n = lax.broadcasted_iota(jnp.int32, (64, 128), 0)
    k2 = (n // 2 % 2) * 32 + (n // 4 % 4) * 8 + (n % 2) * 4 + n // 16
    lane = lax.broadcasted_iota(jnp.int32, (64, 128), 1)
    scaled = (k2 * 128 + lane).astype(F32) / NF
    kerr = 0.2 * scaled
    plasma = 0.5 / (1.0 + 64.0 * scaled * scaled)
    for h in range(2):
        mixed = [[], []]
        for pair in range(2):
            parts = []
            for s in range(3):
                lanes = slice((s * 8 + h * 4 + pair * 2) * 128, (s * 8 + h * 4 + pair * 2 + 2) * 128)
                both = dot(two_ref[...], high_ref[:, lanes])
                rest = dot(two_ref[:128], low_ref[:, lanes])
                parts.append(both[:128] + both[128:] + rest)
            for n in range(2):
                (base_re, base_im), (kerr_re, kerr_im), (plasma_re, plasma_im) = [
                    (part[:64, cuts[n]], part[64:, cuts[n]]) for part in parts
                ]
                mixed[0].append(base_re - kerr * kerr_im - plasma * plasma_re)
                mixed[1].append(base_im + kerr * kerr_re - plasma * plasma_im)
        for part in range(2):
            for c, value in enumerate(exchange_blocks(mixed[part])):
                for z in range(4):
                    start = z * 256 + c // 2 * 128 + c % 2 * 4 + part * 2 + h
                    out_ref[pl.ds(start, 16, stride=8), :] = value[z * 16 : z * 16 + 16]


GROUP = 1


def fft4(values):
    (ar, ai), (br, bi), (cr, ci), (dr, di) = values
    sr, si, tr, ti = ar + cr, ai + ci, ar - cr, ai - ci
    ur, ui, vr, vi = br + dr, bi + di, br - dr, bi - di
    return [(sr + ur, si + ui), (tr + vi, ti - vr), (sr - ur, si - ui), (tr - vi, ti + vr)]


def fft16(values):
    columns = []
    for n in range(4):
        column = fft4([values[4 * m + n] for m in range(4)])
        turned = []
        for k, (re, im) in enumerate(column):
            step = n * k
            if step == 0:
                turned.append((re, im))
            elif step == 4:
                turned.append((im, -re))
            else:
                c = math.cos(2 * math.pi * step / 16)
                s = math.sin(2 * math.pi * step / 16)
                turned.append((re * c + im * s, im * c - re * s))
        columns.append(turned)
    result = [None] * 16
    for k in range(4):
        for m, value in enumerate(fft4([columns[n][k] for n in range(4)])):
            result[k + 4 * m] = value
    return result


def cos_sin(angle):
    quarter = jnp.round(angle * (2.0 / math.pi))
    rest = angle - quarter * 1.5703125
    rest = rest - quarter * 4.837512969970703125e-4
    rest = rest - quarter * 7.54978995489188216e-8
    square = rest * rest
    sine = rest + rest * square * (
        -1.6666654611e-1 + square * (8.3321608736e-3 + square * -1.9515295891e-4)
    )
    cosine = (
        1.0
        - 0.5 * square
        + square
        * square
        * (4.166664568298827e-2 + square * (-1.388731625493765e-3 + square * 2.443315711809948e-5))
    )
    which = quarter.astype(jnp.int32) & 3
    odd = (which & 1) == 1
    cos_out = jnp.where(odd, sine, cosine)
    sin_out = jnp.where(odd, cosine, sine)
    cos_out = jnp.where((which == 1) | (which == 2), -cos_out, cos_out)
    sin_out = jnp.where(which >= 2, -sin_out, sin_out)
    return cos_out, sin_out


def prepare_kernel(screen_ref, strength_ref, phase_ref):
    screen = jnp.broadcast_to(jnp.concatenate([screen_ref[...]] * 2, 1), (8, 128))
    first_point = lax.axis_index("tm") * 8
    mine = 2.0 * pltpu.roll(screen, (128 - first_point) % 128, 1)
    for p in range(8):
        strength_ref[p : p + 1, :] = jnp.broadcast_to(mine[:1, p : p + 1], (1, 128))
    first_bin = lax.axis_index(("tm", "row")) * 32
    bins = lax.broadcasted_iota(jnp.int32, (8, 128), 0)
    lane = lax.broadcasted_iota(jnp.int32, (8, 128), 1)
    for tile in range(4):
        scaled = (first_bin + tile * 8 + bins).astype(F32) / NF
        forward = 40.0 * scaled * (1.0 + 0.3 * scaled * scaled)
        for m in range(16):
            q = lane + m * 128
            transverse = jnp.where(q < NX // 2, q, q - NX).astype(F32) / (NX // 2)
            angle = forward - 20.0 * transverse * transverse / (scaled + 0.05)
            for part, value in enumerate(cos_sin(angle)):
                phase_ref[part, pl.ds(tile * 8, 8), m * 128 : (m + 1) * 128] = value


def cross_kernel(x_ref, phase_ref, table_ref, twist_ref, out_ref, done_ref, sem):
    blocks = []
    for part in range(2):
        for odd in range(2):
            for h in range(2):
                j = part * 2 + h
                pieces = [
                    x_ref[pl.ds((2 * pair + odd) * 32 + j, 8, stride=4), :] for pair in range(16)
                ]
                blocks.append(jnp.concatenate(pieces, 0).T)
    copies = []
    for tile in range(4):
        rows = [slice(n * 32 + tile * 8, n * 32 + tile * 8 + 8) for n in range(4)]
        grid = jnp.concatenate(
            [
                jnp.concatenate([blocks[part * 4 + n // 4][rows[n % 4]] for n in range(16)], 0)
                for part in range(2)
            ],
            1,
        )
        high, low = split(grid)
        first = dot(high, table_ref[0]) + dot(low, table_ref[0]) + dot(high, table_ref[1])
        values = []
        for n in range(16):
            re = first[n * 8 : n * 8 + 8, :128]
            im = first[n * 8 : n * 8 + 8, 128:]
            c = twist_ref[0, n : n + 1, :]
            s = twist_ref[1, n : n + 1, :]
            values.append((re * c + im * s, im * c - re * s))
        rows = pl.ds(tile * 8, 8)
        for m, (re, im) in enumerate(fft16(values)):
            lanes = slice(m * 128, (m + 1) * 128)
            c = phase_ref[0, rows, lanes]
            s = phase_ref[1, rows, lanes]
            done_ref[0, rows, lanes] = re * c - im * s
            done_ref[1, rows, lanes] = re * s + im * c
        copy = pltpu.make_async_copy(done_ref.at[:, rows], out_ref.at[:, rows], sem.at[tile])
        copy.start()
        copies.append(copy)
    for copy in copies:
        copy.wait()


def prepare_part(screen):
    in_vmem = pl.BlockSpec(memory_space=pltpu.VMEM)
    return pl.pallas_call(
        prepare_kernel,
        out_shape=[
            jax.ShapeDtypeStruct((8, 128), F32),
            jax.ShapeDtypeStruct((2, 32, NX), F32),
        ],
        in_specs=[in_vmem],
        out_specs=[in_vmem, in_vmem],
        cost_estimate=pl.CostEstimate(flops=4000000, bytes_accessed=524288, transcendentals=0),
        compiler_params=pltpu.CompilerParams(vmem_limit_bytes=16 * 2**20),
        name="prepare",
    )(screen)


def time_part(strength, samples):
    tables = time_tables()
    in_vmem = pl.BlockSpec(memory_space=pltpu.VMEM)
    return pl.pallas_call(
        time_kernel,
        out_shape=jax.ShapeDtypeStruct((1024, 128), F32),
        in_specs=[in_vmem] * 7,
        out_specs=in_vmem,
        scratch_shapes=[pltpu.VMEM((1024, 128), F32)] + [pltpu.VMEM((256, 3072), BF16)] * 2,
        compiler_params=pltpu.CompilerParams(vmem_limit_bytes=32 * 2**20),
        name="time_spectra",
    )(strength, samples, *tables)


def cross_part(blocks, phases):
    tables = cross_tables()
    in_vmem = pl.BlockSpec(memory_space=pltpu.VMEM)
    return pl.pallas_call(
        cross_kernel,
        out_shape=jax.ShapeDtypeStruct((2, 32, NX), F32),
        in_specs=[in_vmem] * 4,
        out_specs=pl.BlockSpec(memory_space=pl.ANY),
        scratch_shapes=[
            pltpu.VMEM((2, 32, NX), F32),
            pltpu.SemaphoreType.DMA((4,)),
        ],
        compiler_params=pltpu.CompilerParams(vmem_limit_bytes=32 * 2**20),
        name="cross_spectra",
    )(blocks, phases, *tables)


def per_device(field, screen):
    mine = field.reshape(8, 8, 16, 128).transpose(0, 2, 1, 3)
    samples = lax.all_to_all(mine, "tm", split_axis=0, concat_axis=0, tiled=True)
    strength, phases = prepare_part(screen)
    mixed = time_part(strength, samples.reshape(1024, 128))
    blocks = lax.all_to_all(
        mixed.reshape(256, 4, 128),
        ("tm", "row"),
        split_axis=0,
        concat_axis=0,
        axis_index_groups=[device_at().tolist()],
        tiled=True,
    )
    return cross_part(blocks.reshape(1024, 128), phases).reshape(2, 1, 32, NX)


def solution(mesh):
    return jax.shard_map(
        per_device,
        mesh=mesh,
        in_specs=(P(None, "row", "tm"), P(None, "row")),
        out_specs=P(None, None, ("tm", "row"), None),
        check_vma=False,
    )
```
